256 devices in a mesh: blk: 64 (over x_hi, z, y), head: 4 (over x_lo, core).
Axes of the slice: x: 4 (x_hi: 2, x_lo: 2; x = x_hi * 2 + x_lo), y: 4, z: 8, core: 2. Of those that a mesh axis runs over, the one named last changes fastest.
Arguments:
- context_q: bfloat16 [8192, 8192], P('blk', 'head'), may hold values from -200 to 200
- context_k: bfloat16 [8192, 1024], P('blk', 'head'), may hold values from -6 to 6
- context_v: bfloat16 [8192, 1024], P('blk', 'head'), may hold values from -6 to 6
- anchor_k: bfloat16 [1024, 1024], P('blk', 'head'), may hold values from -6 to 6
- anchor_v: bfloat16 [1024, 1024], P('blk', 'head'), may hold values from -6 to 6
- parent_q: bfloat16 [256, 8192], P('blk', 'head'), may hold values from -200 to 200
- block_of_slot: int32 [64], replicated, may hold values from 0 to 63, each once
- agent_lengths: int32 [8], replicated, may hold values from 1 to 2048, 8192 in all
- query_pos: int32 [256], replicated, may hold values from 1 to 8192
Outputs:
- context_out: bfloat16 [8192, 8192], P('blk', 'head')
- parent_out: bfloat16 [256, 8192], P(('blk', 'head'))
The draws below stay inside these ranges and needn't reach their ends.
All inputs are finite; a program needn't handle non-finite values.
Results may differ from the reference program's by a relative error of at most 0.008.
Values may be sent and summed in bfloat16 or wider, within the bound.
No kernel may reach another device: no remote copies, remote signals or barrier semaphores. Data moves between devices by JAX's collectives and lax.ppermute only.
A program may use at most 64 MiB of HBM per device.

```python
import math
import jax
import jax.numpy as jnp
import numpy as np
from jax import lax

HEADS = 64
KV = 8
HD = 128
TOK_DEV = 128
ANCHOR = 1024
AGENTS = 8
BLOCKS = 64
TOKENS = 8192
PARENT = 256


def draw_context_q(key, part):
    key = jax.random.fold_in(key, 11)
    base = jax.random.fold_in(key, 0)
    values = jnp.clip(jax.random.normal(base, (TOKENS, HEADS * HD), jnp.float32), -6.0, 6.0)
    scales = jnp.full((TOKENS, 1), 2.0, jnp.float32)
    return (values * scales).astype(jnp.bfloat16)


def draw_parent_q(key, part):
    key = jax.random.fold_in(key, 23)
    base = jax.random.fold_in(key, 0)
    values = jnp.clip(jax.random.normal(base, (PARENT, HEADS * HD), jnp.float32), -6.0, 6.0)
    scales = jnp.full((PARENT, 1), 2.0, jnp.float32)
    return (values * scales).astype(jnp.bfloat16)


def touch_ends(values, stream_key, least, largest):
    longest = values.shape.index(max(values.shape))
    spots = []
    for shift in (0, 1):
        where = [jax.random.randint(jax.random.fold_in(stream_key, axis), (), 0, length) for axis, length in enumerate(values.shape)]
        where[longest] = (where[longest] + shift) % values.shape[longest]
        spots.append(tuple(where))
    return values.at[spots[0]].set(least).at[spots[1]].set(largest)


def shard_levels(rng, extent, shards, low, top_value):
    def one(dim, shards_of):
        draws = jax.random.uniform(jax.random.fold_in(jax.random.fold_in(rng, 6), dim), (shards_of,), jnp.float32, low / len(shards), top_value / len(shards))
        return jnp.repeat(jnp.exp(draws), extent[dim] // shards_of).reshape((-1,) + (1,) * (len(extent) - dim - 1))

    gain = one(*shards[0])
    for cut in shards[1:]:
        gain = gain * one(*cut)
    return gain


def length_profile(count, total, limit, lean):
    portions = [(1 << 20) // math.isqrt(grade ** lean) + 1 for grade in range(2, count + 1)]
    surplus, holding = total - limit - (count - 1), [1] * (count - 1)
    while surplus > 0:
        movable = [i for i in range(count - 1) if holding[i] < limit]
        pool, budget = sum([portions[i] for i in movable]), surplus
        for i in movable:
            addition = min(limit - holding[i], max(1, budget * portions[i] // pool), surplus)
            holding[i] = holding[i] + addition
            surplus = surplus - addition
    return np.array([limit] + holding)


def uneven_parts(key, amount, total, most, slope):
    if amount == 2:
        one = jax.random.randint(key, (), max(1, total - most), min(most, total - 1) + 1)
        return jnp.stack([one, total - one])
    tallies = jnp.asarray(length_profile(amount, total, most, slope), jnp.int32)
    couples = (amount - 1) // 2
    donor, taker = tallies[1:1 + 2 * couples:2], tallies[2:2 + 2 * couples:2]
    slack = jnp.minimum(donor - 1, most - taker)
    moved = jax.random.randint(jax.random.fold_in(key, 1), (couples,), 0, 1 << 20) % (slack + 1)
    tallies = tallies.at[1:1 + 2 * couples:2].set(donor - moved).at[2:2 + 2 * couples:2].set(taker + moved)
    return tallies[jax.random.permutation(jax.random.fold_in(key, 2), amount)]


def centred(key, extent, scale, reach, cuts=(), kind=jnp.bfloat16):
    array = jax.random.normal(key, extent, jnp.float32) * scale
    if len(cuts) > 0:
        array = shard_levels(key, extent, cuts, -0.22, 0.18) * array
    return jnp.clip(array, min=-reach, max=reach).astype(kind)


def setup_inputs(seed: int = 0) -> dict:
    key_list = jax.random.split(jax.random.key(seed), 10)
    return {
        "context_q": draw_context_q(jax.random.fold_in(key_list[9], 71), 0),
        "context_k": centred(key_list[1], (TOKENS, KV * HD), 1.0, 6.0, ((0, 64), (1, 4))),
        "context_v": centred(key_list[2], (TOKENS, KV * HD), 1.0, 6.0, ((0, 64), (1, 4))),
        "anchor_k": centred(key_list[3], (ANCHOR, KV * HD), 1.0, 6.0, ((0, 64), (1, 4))),
        "anchor_v": centred(key_list[4], (ANCHOR, KV * HD), 1.0, 6.0, ((0, 64), (1, 4))),
        "parent_q": draw_parent_q(jax.random.fold_in(key_list[9], 71), 0),
        "block_of_slot": jax.random.permutation(key_list[6], BLOCKS).astype(jnp.int32),
        "agent_lengths": uneven_parts(key_list[7], AGENTS, TOKENS, TOKENS // 4, 1).astype(jnp.int32),
        "query_pos": touch_ends(jax.random.randint(key_list[8], (PARENT,), 1, TOKENS + 1), jax.random.fold_in(key_list[8], 1), 1, TOKENS).astype(jnp.int32),
    }


def agent_of(positions, agent_lengths):
    ends = jnp.cumsum(agent_lengths).astype(jnp.int32)
    return lax.optimization_barrier(jnp.sum((positions[:, None] >= ends[None, :]).astype(jnp.int32), axis=1)).astype(jnp.int32)

def attend(queries, keys, values, visible):
    scale = 1.0 / math.sqrt(HD)
    scores = jnp.einsum('qgjd,kgd->qgjk', queries, keys) * scale
    scores = jnp.where(visible[:, None, None, :], scores, -jnp.inf)
    peak = lax.optimization_barrier(jnp.max(scores, axis=-1, keepdims=True))
    expo = jnp.exp(scores - peak)
    total = lax.optimization_barrier(jnp.sum(expo, axis=-1))
    weights = lax.optimization_barrier(expo.astype(jnp.bfloat16)).astype(jnp.float32)
    summed = jnp.einsum('qgjk,kgd->qgjd', weights, values)
    return summed / total[..., None]

def reference(context_q, context_k, context_v, anchor_k, anchor_v, parent_q, block_of_slot, agent_lengths, query_pos):
    slots = TOKENS // TOK_DEV
    per_group = HEADS // KV
    offsets = jnp.arange(TOK_DEV, dtype=jnp.int32)
    positions = (block_of_slot[:, None].astype(jnp.int32) * TOK_DEV + offsets[None, :]).astype(jnp.int32)
    flat_pos = positions.reshape(TOKENS)
    agents = agent_of(flat_pos, agent_lengths).reshape(slots, TOK_DEV)
    anchor_keys = anchor_k.astype(jnp.float32).reshape(ANCHOR, KV, HD)
    anchor_vals = anchor_v.astype(jnp.float32).reshape(ANCHOR, KV, HD)

    def one_slot(index):
        start = (index * TOK_DEV).astype(jnp.int32)
        queries = lax.dynamic_slice_in_dim(context_q, start, TOK_DEV, 0).astype(jnp.float32).reshape(TOK_DEV, KV, per_group, HD)
        keys = lax.dynamic_slice_in_dim(context_k, start, TOK_DEV, 0).astype(jnp.float32).reshape(TOK_DEV, KV, HD)
        values = lax.dynamic_slice_in_dim(context_v, start, TOK_DEV, 0).astype(jnp.float32).reshape(TOK_DEV, KV, HD)
        place = positions[index]
        agent = agents[index]
        inside = (place[None, :] <= place[:, None]) & (agent[None, :] == agent[:, None])
        visible = jnp.concatenate([jnp.ones((TOK_DEV, ANCHOR), bool), inside], axis=1)
        result = attend(queries, jnp.concatenate([anchor_keys, keys], 0), jnp.concatenate([anchor_vals, values], 0), visible)
        return result.reshape(TOK_DEV, HEADS * HD).astype(jnp.bfloat16)
    context_out = lax.map(one_slot, jnp.arange(slots, dtype=jnp.int32)).reshape(TOKENS, HEADS * HD)
    key_pos = jnp.concatenate([jnp.full((ANCHOR,), -1, jnp.int32), flat_pos])
    visible = key_pos[None, :] < query_pos[:, None]
    all_keys = jnp.concatenate([anchor_keys, context_k.astype(jnp.float32).reshape(TOKENS, KV, HD)], 0)
    all_vals = jnp.concatenate([anchor_vals, context_v.astype(jnp.float32).reshape(TOKENS, KV, HD)], 0)
    group_q = jnp.transpose(parent_q.astype(jnp.float32).reshape(PARENT, KV, per_group, HD), (1, 0, 2, 3))
    group_k = jnp.transpose(all_keys, (1, 0, 2))
    group_v = jnp.transpose(all_vals, (1, 0, 2))

    def one_group(items):
        queries, keys, values = items
        return attend(queries[:, None], keys[:, None], values[:, None], visible)[:, 0]
    outs = lax.map(one_group, (group_q, group_k, group_v))
    parent_out = jnp.transpose(outs, (1, 0, 2, 3)).reshape(PARENT, HEADS * HD).astype(jnp.bfloat16)
    return (context_out, parent_out)
```

```python
import functools
import math

import jax
import jax.numpy as jnp
from jax import lax
from jax.experimental import pallas as pl
from jax.experimental.pallas import tpu as pltpu
from jax.sharding import Mesh
from jax.sharding import PartitionSpec as P

HD = 128
NX, NZ, NY, NL, NC = 2, 8, 4, 2, 2
NB = NX * NZ
NH = NL * NC
GROUPS = 2
PER = 8
GH = GROUPS * PER
TOK = 128
ANC = 16
QR = 4
KVR = TOK + ANC
KEYS = 640
STRIDE = 4 * ANC
LOG2E = 1.4426950408889634
SCALE = LOG2E / math.sqrt(HD)
BF = jnp.bfloat16
F32 = jnp.float32
VMEM = pl.BlockSpec(memory_space=pltpu.VMEM)
SMEM = pl.BlockSpec(memory_space=pltpu.SMEM)


def params():
    return pltpu.CompilerParams(vmem_limit_bytes=40 * 1024 * 1024)


def nt(a, b):
    return lax.dot_general(a, b, (((1,), (1,)), ((), ())), preferred_element_type=F32)


def prep_kernel(ak, av, pq, ck, cv, send, kv, scr):
    q = pq[...].astype(F32)
    for g in range(GROUPS):
        for r in range(QR):
            for h in range(PER):
                col = (g * PER + h) * HD
                row = (g * QR + r) * PER + h
                scr[row : row + 1, :] = q[r : r + 1, col : col + HD]
    parts = [ak[:, :HD], ak[:, HD:], av[:, :HD], av[:, HD:]]
    chunk = jnp.concatenate(parts + [scr[...].astype(BF)], 0)
    for b in range(NB):
        send[b] = chunk
    ctx = [ck[:, :HD], ck[:, HD:], cv[:, :HD], cv[:, HD:]]
    for i in range(4):
        kv[i, :TOK, :] = ctx[i]
        kv[i, TOK:, :] = parts[i]


def parent_kernel(bos, qp, got, kv0, kv1, kv2, kv3, out, stat, keys, vals, qpos):
    slot = (lax.axis_index("xh") * NZ + lax.axis_index("z")) * NY
    y = lax.axis_index("y")
    blocks = [kv0, kv1, kv2, kv3]
    pad = jnp.zeros((KEYS - NY * KVR, HD), BF)
    for g in range(GROUPS):
        for i in range(NY):
            keys[g, i * TOK : (i + 1) * TOK, :] = blocks[i][g, :TOK, :]
            vals[g, i * TOK : (i + 1) * TOK, :] = blocks[i][2 + g, :TOK, :]
            at = NY * TOK + i * ANC
            keys[g, at : at + ANC, :] = blocks[i][g, TOK:, :]
            vals[g, at : at + ANC, :] = blocks[i][2 + g, TOK:, :]
        keys[g, NY * KVR :, :] = pad
        vals[g, NY * KVR :, :] = pad
    for b in range(NB):
        for r in range(QR):
            row = (b * QR + r) * PER
            qpos[row : row + PER, :] = jnp.full((PER, HD), qp[(b * NY + y) * QR + r], jnp.int32)
    lane = lax.broadcasted_iota(jnp.int32, (1, KEYS), 1)
    kpos = jnp.where(lane < NY * KVR, -1, 1 << 30)
    for i in range(NY):
        src = slot + lax.rem(y + NY - i, NY)
        base = bos[src] * TOK - i * TOK
        kpos = jnp.where((lane >= i * TOK) & (lane < (i + 1) * TOK), lane + base, kpos)
    visible = kpos < qpos[:, :1]
    rows = NB * QR * PER
    parts, stats = [], jnp.zeros((NB * QR, HD), F32)
    lanes = lax.broadcasted_iota(jnp.int32, (1, PER, HD), 2)
    heads = lax.broadcasted_iota(jnp.int32, (1, PER, HD), 1)
    for g in range(GROUPS):
        lo = STRIDE + g * QR * PER
        q = got[:, lo : lo + QR * PER, :].reshape(rows, HD)
        s = nt(q, keys[g]) * SCALE
        s = jnp.where(visible, s, -1e30)
        m = jnp.max(s, axis=1, keepdims=True)
        p = jnp.exp2(s - m)
        total = jnp.sum(p, axis=1, keepdims=True)
        o = jnp.dot(p.astype(BF), vals[g], preferred_element_type=F32)
        o = o / total
        parts.append(o.reshape(NB * QR, PER, HD))
        lse = m + jnp.log2(total)
        hi = lse.astype(BF).astype(F32)
        mid = (lse - hi).astype(BF).astype(F32)
        low = lse - hi - mid
        pick = lanes - g * PER
        for k, part in enumerate((hi, mid, low)):
            wide = jnp.broadcast_to(part, (rows, HD)).reshape(NB * QR, PER, HD)
            stats = stats + jnp.sum(jnp.where(pick - k * GH == heads, wide, 0.0), axis=1)
    out[...] = jnp.concatenate(parts, 1).astype(BF)
    stat[...] = stats.astype(BF)


def context_kernel(bos, lens, q_ref, ck, cv, a0, a1, a2, a3, out, keys, vals):
    slot = (lax.axis_index("xh") * NZ + lax.axis_index("z")) * NY + lax.axis_index("y")
    base = bos[slot] * TOK
    count = NB * ANC
    for i, a in enumerate((a0, a1, a2, a3)):
        for g in range(GROUPS):
            k, v = g * ANC, (GROUPS + g) * ANC
            keys[g, i * count : (i + 1) * count, :] = a[:, k : k + ANC, :].reshape(count, HD)
            vals[g, i * count : (i + 1) * count, :] = a[:, v : v + ANC, :].reshape(count, HD)
    mine = lax.broadcasted_iota(jnp.int32, (TOK, TOK), 0)
    other = lax.broadcasted_iota(jnp.int32, (TOK, TOK), 1)
    visible = other <= mine
    end = jnp.int32(0)
    for j in range(lens.shape[0]):
        end = end + lens[j]
        visible = visible & ((mine + base >= end) == (other + base >= end))
    for g in range(GROUPS):
        own_k = ck[:, g * HD : (g + 1) * HD]
        own_v = cv[:, g * HD : (g + 1) * HD]
        for half in range(4):
            hs = [g * PER + half * 2 + j for j in range(2)]
            q = jnp.concatenate([q_ref[:, h * HD : (h + 1) * HD] for h in hs], 0)
            sa = nt(q, keys[g]) * SCALE
            so = nt(q, own_k) * SCALE
            so = jnp.where(visible[None], so.reshape(2, TOK, TOK), -1e30).reshape(2 * TOK, TOK)
            m = jnp.maximum(jnp.max(sa, axis=1, keepdims=True), jnp.max(so, axis=1, keepdims=True))
            pa = jnp.exp2(sa - m)
            po = jnp.exp2(so - m)
            total = jnp.sum(pa, axis=1, keepdims=True) + jnp.sum(po, axis=1, keepdims=True)
            o = jnp.dot(pa.astype(BF), vals[g], preferred_element_type=F32)
            o = o + jnp.dot(po.astype(BF), own_v, preferred_element_type=F32)
            o = (o / total).astype(BF)
            for j, h in enumerate(hs):
                out[:, h * HD : (h + 1) * HD] = o[j * TOK : (j + 1) * TOK]


def combine_kernel(got, out):
    st = got[:, GH * HD :].astype(F32)
    lse = st + pltpu.roll(st, HD - GH, 1) + pltpu.roll(st, HD - 2 * GH, 1)
    tiles = lse.reshape(NB * NH // 8, 8, HD)
    top = jnp.max(tiles, axis=0)
    top = jnp.maximum(top, pltpu.roll(top, 4, 0))
    w = jnp.exp2(tiles - top[None])
    total = jnp.sum(w, axis=0)
    total = total + pltpu.roll(total, 4, 0)
    w = (w / total[None]).reshape(NB * NH, HD)
    for h in range(GH):
        x = got[:, h * HD : (h + 1) * HD].astype(F32) * w[:, h : h + 1]
        x = jnp.sum(x.reshape(NB * NH // 8, 8, HD), axis=0)
        x = x + pltpu.roll(x, 4, 0)
        for k in range(NH):
            at = (k * GH + h) * HD
            out[:, at : at + HD] = x[k : k + 1].astype(BF)


def on_device(cq, ck, cv, ak, av, pq, bos, lens, qp):
    send, kv = pl.pallas_call(
        prep_kernel,
        out_shape=(
            jax.ShapeDtypeStruct((NB, 2 * STRIDE, HD), BF),
            jax.ShapeDtypeStruct((4, KVR, HD), BF),
        ),
        in_specs=[VMEM] * 5,
        out_specs=(VMEM, VMEM),
        scratch_shapes=[pltpu.VMEM((STRIDE, HD), F32)],
        compiler_params=params(),
        name="prep",
    )(ak, av, pq, ck, cv)

    def turn(x, shift):
        return lax.ppermute(x, "y", [(i, (i + shift) % NY) for i in range(NY)])

    kvs = [kv] + [turn(kv, s) for s in (1, 2, 3)]
    got = lax.all_to_all(send, ("xh", "z"), 0, 0, tiled=True)
    anchors = got[:, :STRIDE]
    anchors = [anchors] + [turn(anchors, s) for s in (1, 2, 3)]
    part, stat = pl.pallas_call(
        parent_kernel,
        out_shape=(
            jax.ShapeDtypeStruct((NB * QR, GH, HD), BF),
            jax.ShapeDtypeStruct((NB * QR, HD), BF),
        ),
        in_specs=[SMEM] * 2 + [VMEM] * 5,
        out_specs=(VMEM, VMEM),
        scratch_shapes=[
            pltpu.VMEM((GROUPS, KEYS, HD), BF),
            pltpu.VMEM((GROUPS, KEYS, HD), BF),
            pltpu.VMEM((NB * QR * PER, HD), jnp.int32),
        ],
        compiler_params=params(),
        cost_estimate=pl.CostEstimate(flops=10**9, bytes_accessed=2 * 10**6, transcendentals=10**6),
        name="parent",
    )(bos, qp, got, *kvs)
    packed = jnp.concatenate([part.reshape(NB * QR, GH * HD), stat], 1)
    back = lax.all_to_all(packed, ("xh", "z", "xl", "c"), 0, 0, tiled=True)
    context = pl.pallas_call(
        context_kernel,
        out_shape=jax.ShapeDtypeStruct((TOK, GH * HD), BF),
        in_specs=[SMEM] * 2 + [VMEM] * 7,
        out_specs=VMEM,
        scratch_shapes=[
            pltpu.VMEM((GROUPS, NY * NB * ANC, HD), BF),
            pltpu.VMEM((GROUPS, NY * NB * ANC, HD), BF),
        ],
        compiler_params=params(),
        cost_estimate=pl.CostEstimate(flops=3 * 10**9, bytes_accessed=4 * 10**6, transcendentals=3 * 10**6),
        name="context",
    )(bos, lens, cq, ck, cv, *anchors)
    parent = pl.pallas_call(
        combine_kernel,
        out_shape=jax.ShapeDtypeStruct((1, NH * GH * HD), BF),
        in_specs=[VMEM],
        out_specs=VMEM,
        compiler_params=params(),
        name="combine",
    )(back)
    return context, parent


def solution(mesh):
    fine = Mesh(mesh.devices.reshape(NX, NZ, NY, NL, NC), ("xh", "z", "y", "xl", "c"))
    blk, head = ("xh", "z", "y"), ("xl", "c")
    both = P(blk, head)
    return jax.shard_map(
        on_device,
        mesh=fine,
        in_specs=(both,) * 6 + (P(), P(), P()),
        out_specs=(both, P(blk + head, None)),
        check_vma=False,
    )
```

```python
import functools
import math

import jax
import jax.numpy as jnp
from jax import lax
from jax.experimental import pallas as pl
from jax.experimental.pallas import tpu as pltpu
from jax.sharding import Mesh
from jax.sharding import PartitionSpec as P

HD = 128
NX, NZ, NY, NL, NC = 2, 8, 4, 2, 2
NB = NX * NZ
NH = NL * NC
GROUPS = 2
PER = 8
GH = GROUPS * PER
TOK = 128
ANC = 16
QR = 4
KVR = TOK + ANC
KEYS = 640
STRIDE = 4 * ANC
LOG2E = 1.4426950408889634
WIDE = PER * HD + HD
SCALE = LOG2E / math.sqrt(HD)
BF = jnp.bfloat16
F32 = jnp.float32
VMEM = pl.BlockSpec()
SMEM = pl.BlockSpec(memory_space=pltpu.SMEM)


def params(mib=40):
    return pltpu.CompilerParams(vmem_limit_bytes=mib * 1024 * 1024)


def nt(a, b):
    return lax.dot_general(a, b, (((1,), (1,)), ((), ())), preferred_element_type=F32)


def prep_kernel(ak, av, pq, ck, cv, send, kv, scr):
    q = pq[...].astype(F32)
    for g in range(GROUPS):
        for r in range(QR):
            for h in range(PER):
                col = (g * PER + h) * HD
                row = (g * QR + r) * PER + h
                scr[row : row + 1, :] = q[r : r + 1, col : col + HD]
    parts = [ak[:, :HD], ak[:, HD:], av[:, :HD], av[:, HD:]]
    chunk = jnp.concatenate(parts + [scr[...].astype(BF)], 0)
    for b in range(NB):
        send[b] = chunk
    ctx = [ck[:, :HD], ck[:, HD:], cv[:, :HD], cv[:, HD:]]
    for i in range(4):
        kv[i, :TOK, :] = ctx[i]
        kv[i, TOK:, :] = parts[i]


def parent_kernel(bos, qp, got, kv0, kv1, kv2, kv3, out, keys, vals, qpos, turned):
    slot = (lax.axis_index("xh") * NZ + lax.axis_index("z")) * NY
    y = lax.axis_index("y")
    blocks = [kv0, kv1, kv2, kv3]
    pad = jnp.zeros((KEYS - NY * KVR, HD), BF)
    for g in range(GROUPS):
        for i in range(NY):
            keys[g, i * TOK : (i + 1) * TOK, :] = blocks[i][g, :TOK, :]
            vals[g, i * TOK : (i + 1) * TOK, :] = blocks[i][2 + g, :TOK, :]
            at = NY * TOK + i * ANC
            keys[g, at : at + ANC, :] = blocks[i][g, TOK:, :]
            vals[g, at : at + ANC, :] = blocks[i][2 + g, TOK:, :]
        keys[g, NY * KVR :, :] = pad
        vals[g, NY * KVR :, :] = pad
    for b in range(NB):
        for r in range(QR):
            row = (b * QR + r) * PER
            qpos[row : row + PER, :] = jnp.full((PER, HD), qp[(b * NY + y) * QR + r], jnp.int32)
    rows = NB * QR * PER
    lane = lax.broadcasted_iota(jnp.int32, (rows, HD), 1)
    masks = []
    for i in range(NY):
        base = bos[slot + lax.rem(y + NY - i, NY)] * TOK
        masks.append(lane + base < qpos[...])
    masks.append(lane < NY * ANC)
    stats = jnp.zeros((NB * QR, HD), F32)
    lanes = lax.broadcasted_iota(jnp.int32, (NB * QR, HD), 1)
    for g in range(GROUPS):
        lo = STRIDE + g * QR * PER
        q = got[:, lo : lo + QR * PER, :].reshape(rows, HD)
        s = nt(q, keys[g])
        s = [jnp.where(v, s[:, i * HD : (i + 1) * HD] * SCALE, -1e30) for i, v in enumerate(masks)]
        m = jnp.max(functools.reduce(jnp.maximum, s), axis=1, keepdims=True)
        p = [jnp.exp2(x - m) for x in s]
        total = jnp.sum(sum(p[1:], p[0]), axis=1, keepdims=True)
        p = jnp.concatenate([x.astype(BF) for x in p], 1)
        o = jnp.dot(p, vals[g], preferred_element_type=F32)
        turned[0] = o * (1.0 / total)
        turned[1] = jnp.broadcast_to(m + jnp.log2(total), (rows, HD))
        for h in range(PER):
            col = g * PER + h
            at = g * WIDE + h * HD
            pick = pl.ds(h, NB * QR, stride=PER)
            out[:, at : at + HD] = turned[0, pick, :].astype(BF)
            stats = jnp.where(lanes == col, turned[1, pick, :], stats)
    hi = stats.astype(BF).astype(F32)
    mid = (stats - hi).astype(BF).astype(F32)
    low = stats - hi - mid
    stats = hi + pltpu.roll(mid, GH, 1) + pltpu.roll(low, 2 * GH, 1)
    for g in range(GROUPS):
        out[:, g * WIDE + PER * HD : (g + 1) * WIDE] = stats.astype(BF)


def context_kernel(bos, lens, q_ref, ck, cv, a0, a1, a2, a3, out, keys, vals):
    slot = (lax.axis_index("xh") * NZ + lax.axis_index("z")) * NY + lax.axis_index("y")
    base = bos[slot] * TOK
    count = NB * ANC
    for i, a in enumerate((a0, a1, a2, a3)):
        for g in range(GROUPS):
            k, v = g * ANC, (GROUPS + g) * ANC
            keys[g, i * count : (i + 1) * count, :] = a[:, k : k + ANC, :].reshape(count, HD)
            vals[g, i * count : (i + 1) * count, :] = a[:, v : v + ANC, :].reshape(count, HD)
    mine = lax.broadcasted_iota(jnp.int32, (TOK, TOK), 0)
    other = lax.broadcasted_iota(jnp.int32, (TOK, TOK), 1)
    visible = other <= mine
    end = jnp.int32(0)
    for j in range(lens.shape[0]):
        end = end + lens[j]
        visible = visible & ((mine + base >= end) == (other + base >= end))
    for g in range(GROUPS):
        own_k = ck[:, g * HD : (g + 1) * HD]
        own_v = cv[:, g * HD : (g + 1) * HD]
        for half in range(4):
            hs = [g * PER + half * 2 + j for j in range(2)]
            q = jnp.concatenate([q_ref[:, h * HD : (h + 1) * HD] for h in hs], 0)
            sa = nt(q, keys[g]) * SCALE
            so = nt(q, own_k) * SCALE
            so = jnp.where(visible[None], so.reshape(2, TOK, TOK), -1e30).reshape(2 * TOK, TOK)
            m = jnp.maximum(jnp.max(sa, axis=1, keepdims=True), jnp.max(so, axis=1, keepdims=True))
            pa = jnp.exp2(sa - m)
            po = jnp.exp2(so - m)
            total = jnp.sum(pa, axis=1, keepdims=True) + jnp.sum(po, axis=1, keepdims=True)
            o = jnp.dot(pa.astype(BF), vals[g], preferred_element_type=F32)
            o = o + jnp.dot(po.astype(BF), own_v, preferred_element_type=F32)
            o = (o / total).astype(BF)
            for j, h in enumerate(hs):
                out[:, h * HD : (h + 1) * HD] = o[j * TOK : (j + 1) * TOK]


def combine_kernel(got, out):
    st = got[:, PER * HD : WIDE].astype(F32)
    lse = st + pltpu.roll(st, HD - GH, 1) + pltpu.roll(st, HD - 2 * GH, 1)
    tiles = lse.reshape(NB * NH // 8, 8, HD)
    top = jnp.max(tiles, axis=0)
    top = jnp.maximum(top, pltpu.roll(top, 4, 0))
    w = jnp.exp2(tiles - top[None])
    total = jnp.sum(w, axis=0)
    total = total + pltpu.roll(total, 4, 0)
    w = (w / total[None]).reshape(NB * NH, HD)
    for h in range(GH):
        at = h // PER * WIDE + h % PER * HD
        x = got[:, at : at + HD].astype(F32) * w[:, h : h + 1]
        x = jnp.sum(x.reshape(NB * NH // 8, 8, HD), axis=0)
        x = x + pltpu.roll(x, 4, 0)
        for k in range(NH):
            at = (k * GH + h) * HD
            out[:, at : at + HD] = x[k : k + 1].astype(BF)


def on_device(cq, ck, cv, ak, av, pq, bos, lens, qp):
    send, kv = pl.pallas_call(
        prep_kernel,
        out_shape=(
            jax.ShapeDtypeStruct((NB, 2 * STRIDE, HD), BF),
            jax.ShapeDtypeStruct((4, KVR, HD), BF),
        ),
        in_specs=[VMEM] * 5,
        out_specs=(VMEM, VMEM),
        scratch_shapes=[pltpu.VMEM((STRIDE, HD), F32)],
        compiler_params=params(60),
        name="prep",
    )(ak, av, pq, ck, cv)

    def turn(x, shift):
        return lax.ppermute(x, "y", [(i, (i + shift) % NY) for i in range(NY)])

    kvs = [kv] + [turn(kv, s) for s in (1, 2, 3)]
    got = lax.all_to_all(send, ("xh", "z"), 0, 0, tiled=True)
    got, *kvs = lax.optimization_barrier((got, *kvs))
    anchors = got[:, :STRIDE]
    anchors = [anchors] + [turn(anchors, s) for s in (1, 2, 3)]
    part = pl.pallas_call(
        parent_kernel,
        out_shape=jax.ShapeDtypeStruct((NB * QR, GROUPS * WIDE), BF),
        in_specs=[SMEM] * 2 + [VMEM] * 5,
        out_specs=VMEM,
        scratch_shapes=[
            pltpu.VMEM((GROUPS, KEYS, HD), BF),
            pltpu.VMEM((GROUPS, KEYS, HD), BF),
            pltpu.VMEM((NB * QR * PER, HD), jnp.int32),
            pltpu.VMEM((2, NB * QR * PER, HD), F32),
        ],
        compiler_params=params(),
        cost_estimate=pl.CostEstimate(flops=10**9, bytes_accessed=2 * 10**6, transcendentals=10**6),
        name="parent",
    )(bos, qp, got, *kvs)
    part = part.reshape(NB * QR, GROUPS, WIDE)
    back = lax.all_to_all(part, ("xh", "z", "xl", "c"), 0, 0, tiled=True)
    context = pl.pallas_call(
        context_kernel,
        out_shape=jax.ShapeDtypeStruct((TOK, GH * HD), BF),
        in_specs=[SMEM] * 2 + [VMEM] * 7,
        out_specs=VMEM,
        scratch_shapes=[
            pltpu.VMEM((GROUPS, NY * NB * ANC, HD), BF),
            pltpu.VMEM((GROUPS, NY * NB * ANC, HD), BF),
        ],
        compiler_params=params(),
        cost_estimate=pl.CostEstimate(flops=60 * 10**9, bytes_accessed=4 * 10**6, transcendentals=3 * 10**6),
        name="context",
    )(bos, lens, cq, ck, cv, *anchors)
    parent = pl.pallas_call(
        combine_kernel,
        out_shape=jax.ShapeDtypeStruct((1, NH * GH * HD), BF),
        in_specs=[VMEM],
        out_specs=VMEM,
        compiler_params=params(),
        name="combine",
    )(back.reshape(NB * NH, GROUPS * WIDE))
    return context, parent


def solution(mesh):
    fine = Mesh(mesh.devices.reshape(NX, NZ, NY, NL, NC), ("xh", "z", "y", "xl", "c"))
    blk, head = ("xh", "z", "y"), ("xl", "c")
    both = P(blk, head)
    return jax.shard_map(
        on_device,
        mesh=fine,
        in_specs=(both,) * 6 + (P(), P(), P()),
        out_specs=(both, P(blk + head, None)),
        check_vma=False,
    )
```

```python
import functools
import math

import jax
import jax.numpy as jnp
from jax import lax
from jax.experimental import pallas as pl
from jax.experimental.pallas import tpu as pltpu
from jax.sharding import Mesh
from jax.sharding import PartitionSpec as P

HD = 128
NX, NZ, NY, NL, NC = 2, 8, 4, 2, 2
NB = NX * NZ
NA = NX * NY
NH = NL * NC
GROUPS = 2
PER = 8
GH = GROUPS * PER
TOK = 128
ANC = 16
QR = 4
KVR = TOK + ANC
KEYS = NA * KVR
STRIDE = 4 * ANC
CHUNK = STRIDE + QR * PER
ROWS = NB * QR
LOG2E = 1.4426950408889634
WIDE = PER * HD + 2 * HD
SCALE = LOG2E / math.sqrt(HD)
BF = jnp.bfloat16
F32 = jnp.float32
VMEM = pl.BlockSpec()
SMEM = pl.BlockSpec(memory_space=pltpu.SMEM)


def params(mib=40):
    return pltpu.CompilerParams(vmem_limit_bytes=mib * 1024 * 1024)


def nt(a, b):
    return lax.dot_general(a, b, (((1,), (1,)), ((), ())), preferred_element_type=F32)


def half_kernel(ak, av, ck, cv, keep, give):
    first = lax.axis_index("xh") == 0
    for i, (ctx, anc) in enumerate(((ck, ak), (cv, av))):
        for rows, src in ((slice(0, TOK), ctx), (slice(TOK, KVR), anc)):
            low, high = src[:, :HD], src[:, HD:]
            keep[i, rows, :] = jnp.where(first, low, high)
            give[i, rows, :] = jnp.where(first, high, low)


def send_kernel(ak, av, pq, send, scr):
    q = pq[...].astype(F32)
    for g in range(GROUPS):
        for r in range(QR):
            for h in range(PER):
                col = (g * PER + h) * HD
                row = (g * QR + r) * PER + h
                scr[row : row + 1, :] = q[r : r + 1, col : col + HD]
    parts = [ak[:, :HD], ak[:, HD:], av[:, :HD], av[:, HD:]]
    for x in range(NX):
        lo = x * QR * PER
        chunk = jnp.concatenate(parts + [scr[lo : lo + QR * PER, :].astype(BF)], 0)
        for z in range(NZ):
            send[x * NZ + z] = chunk


def parent_kernel(bos, qp, got, kv0, kv1, kv2, kv3, out, keys, vals, qpos, turned):
    x, z, y = lax.axis_index("xh"), lax.axis_index("z"), lax.axis_index("y")
    masks = []
    for b in range(NB):
        for r in range(QR):
            row = (b * QR + r) * PER
            qpos[row : row + PER, :] = jnp.full((PER, HD), qp[(b * NY + y) * QR + r], jnp.int32)
    rows = ROWS * PER
    lane = lax.broadcasted_iota(jnp.int32, (rows, HD), 1)
    for i, kv in enumerate((kv0, kv1, kv2, kv3)):
        for k in range(NX):
            at = i * NX + k
            keys[at * TOK : (at + 1) * TOK, :] = kv[k, 0, :TOK, :]
            vals[at * TOK : (at + 1) * TOK, :] = kv[k, 1, :TOK, :]
            owner = x if k == 0 else 1 - x
            base = bos[(owner * NZ + z) * NY + lax.rem(y + NY - i, NY)] * TOK
            masks.append(lane + base < qpos[...])
            at = NA * TOK + at * ANC
            keys[at : at + ANC, :] = kv[k, 0, TOK:, :]
            vals[at : at + ANC, :] = kv[k, 1, TOK:, :]
    q = got[:, STRIDE:, :].reshape(rows, HD)
    s = nt(q, keys[...]) * SCALE
    s = [s[:, i * HD : (i + 1) * HD] for i in range(KEYS // HD)]
    s = [jnp.where(v, t, -1e30) for v, t in zip(masks, s)] + s[NA:]
    m = jnp.max(functools.reduce(jnp.maximum, s), axis=1, keepdims=True)
    p = [jnp.exp2(v - m) for v in s]
    total = jnp.sum(sum(p[1:], p[0]), axis=1, keepdims=True)
    p = jnp.concatenate([v.astype(BF) for v in p], 1)
    o = jnp.dot(p, vals[...], preferred_element_type=F32)
    turned[0] = o * (1.0 / total)
    turned[1] = jnp.broadcast_to(m + jnp.log2(total), (rows, HD))
    stats = jnp.zeros((ROWS, HD), F32)
    lanes = lax.broadcasted_iota(jnp.int32, (ROWS, HD), 1)
    for h in range(PER):
        pick = pl.ds(h, ROWS, stride=PER)
        out[:, h * HD : (h + 1) * HD] = turned[0, pick, :].astype(BF)
        stats = jnp.where(lanes == h, turned[1, pick, :], stats)
    hi = stats.astype(BF).astype(F32)
    mid = (stats - hi).astype(BF).astype(F32)
    low = stats - hi - mid
    stats = hi + pltpu.roll(mid, PER, 1) + pltpu.roll(low, 2 * PER, 1)
    out[:, PER * HD : PER * HD + HD] = stats.astype(BF)
    out[:, PER * HD + HD :] = jnp.zeros((ROWS, HD), BF)


def context_kernel(bos, lens, q_ref, ck, cv, a0, a1, a2, a3, out, keys, vals):
    slot = (lax.axis_index("xh") * NZ + lax.axis_index("z")) * NY + lax.axis_index("y")
    base = bos[slot] * TOK
    count = NB * ANC
    for i, a in enumerate((a0, a1, a2, a3)):
        for g in range(GROUPS):
            k, v = g * ANC, (GROUPS + g) * ANC
            keys[g, i * count : (i + 1) * count, :] = a[:, k : k + ANC, :].reshape(count, HD)
            vals[g, i * count : (i + 1) * count, :] = a[:, v : v + ANC, :].reshape(count, HD)
    mine = lax.broadcasted_iota(jnp.int32, (TOK, TOK), 0)
    other = lax.broadcasted_iota(jnp.int32, (TOK, TOK), 1)
    visible = other <= mine
    end = jnp.int32(0)
    for j in range(lens.shape[0]):
        end = end + lens[j]
        visible = visible & ((mine + base >= end) == (other + base >= end))
    for g in range(GROUPS):
        own_k = ck[:, g * HD : (g + 1) * HD]
        own_v = cv[:, g * HD : (g + 1) * HD]
        for half in range(4):
            hs = [g * PER + half * 2 + j for j in range(2)]
            q = jnp.concatenate([q_ref[:, h * HD : (h + 1) * HD] for h in hs], 0)
            sa = nt(q, keys[g]) * SCALE
            so = nt(q, own_k) * SCALE
            so = jnp.where(visible[None], so.reshape(2, TOK, TOK), -1e30).reshape(2 * TOK, TOK)
            m = jnp.maximum(jnp.max(sa, axis=1, keepdims=True), jnp.max(so, axis=1, keepdims=True))
            pa = jnp.exp2(sa - m)
            po = jnp.exp2(so - m)
            total = jnp.sum(pa, axis=1, keepdims=True) + jnp.sum(po, axis=1, keepdims=True)
            o = jnp.dot(pa.astype(BF), vals[g], preferred_element_type=F32)
            o = o + jnp.dot(po.astype(BF), own_v, preferred_element_type=F32)
            o = (o / total).astype(BF)
            for j, h in enumerate(hs):
                out[:, h * HD : (h + 1) * HD] = o[j * TOK : (j + 1) * TOK]


def combine_kernel(got, out):
    st = got[:, PER * HD : PER * HD + HD].astype(F32)
    lse = st + pltpu.roll(st, HD - PER, 1) + pltpu.roll(st, HD - 2 * PER, 1)
    count = NZ * NH // 8
    tiles = lse.reshape(GROUPS, count, 8, HD)
    top = jnp.max(tiles, axis=1)
    top = jnp.maximum(top, pltpu.roll(top, 4, 1))
    w = jnp.exp2(tiles - top[:, None])
    total = jnp.sum(w, axis=1)
    total = total + pltpu.roll(total, 4, 1)
    w = (w / total[:, None]).reshape(GROUPS * NZ * NH, HD)
    for h in range(PER):
        x = got[:, h * HD : (h + 1) * HD].astype(F32) * w[:, h : h + 1]
        x = jnp.sum(x.reshape(GROUPS, count, 8, HD), axis=1)
        x = x + pltpu.roll(x, 4, 1)
        for k in range(NH):
            for g in range(GROUPS):
                at = (k * GH + g * PER + h) * HD
                out[:, at : at + HD] = x[g, k : k + 1].astype(BF)


def on_device(cq, ck, cv, ak, av, pq, bos, lens, qp):
    half = jax.ShapeDtypeStruct((2, KVR, HD), BF)
    keep, give = pl.pallas_call(
        half_kernel,
        out_shape=(half, half),
        in_specs=[VMEM] * 4,
        out_specs=(VMEM,) * 2,
        compiler_params=params(60),
        name="half",
    )(ak, av, ck, cv)
    send = pl.pallas_call(
        send_kernel,
        out_shape=jax.ShapeDtypeStruct((NB, CHUNK, HD), BF),
        in_specs=[VMEM] * 3,
        out_specs=VMEM,
        scratch_shapes=[pltpu.VMEM((GROUPS * QR * PER, HD), F32)],
        compiler_params=params(60),
        cost_estimate=pl.CostEstimate(flops=3 * 10**9, bytes_accessed=10**6, transcendentals=0),
        name="send",
    )(ak, av, pq)

    def turn(x, shift):
        return lax.ppermute(x, "y", [(i, (i + shift) % NY) for i in range(NY)])

    other = lax.ppermute(give, "xh", [(0, 1), (1, 0)])
    send, other = lax.optimization_barrier((send, other))
    kv = jnp.stack([keep, other])
    kvs = [kv] + [turn(kv, s) for s in (1, 2, 3)]
    got = lax.all_to_all(send, ("xh", "z"), 0, 0, tiled=True)
    got, *kvs = lax.optimization_barrier((got, *kvs))
    anchors = got[:, :STRIDE]
    anchors = [anchors] + [turn(anchors, s) for s in (1, 2, 3)]
    part = pl.pallas_call(
        parent_kernel,
        out_shape=jax.ShapeDtypeStruct((ROWS, WIDE), BF),
        in_specs=[SMEM] * 2 + [VMEM] * 5,
        out_specs=VMEM,
        scratch_shapes=[
            pltpu.VMEM((KEYS, HD), BF),
            pltpu.VMEM((KEYS, HD), BF),
            pltpu.VMEM((ROWS * PER, HD), jnp.int32),
            pltpu.VMEM((2, ROWS * PER, HD), F32),
        ],
        compiler_params=params(),
        cost_estimate=pl.CostEstimate(flops=10**9, bytes_accessed=2 * 10**6, transcendentals=10**6),
        name="parent",
    )(bos, qp, got, *kvs)
    part = part.reshape(ROWS, 2, WIDE // 2)
    back = lax.all_to_all(part, ("xh", "z", "xl", "c"), 0, 0, tiled=True)
    context = pl.pallas_call(
        context_kernel,
        out_shape=jax.ShapeDtypeStruct((TOK, GH * HD), BF),
        in_specs=[SMEM] * 2 + [VMEM] * 7,
        out_specs=VMEM,
        scratch_shapes=[
            pltpu.VMEM((GROUPS, NY * NB * ANC, HD), BF),
            pltpu.VMEM((GROUPS, NY * NB * ANC, HD), BF),
        ],
        compiler_params=params(),
        cost_estimate=pl.CostEstimate(flops=60 * 10**9, bytes_accessed=4 * 10**6, transcendentals=3 * 10**6),
        name="context",
    )(bos, lens, cq, ck, cv, *anchors)
    parent = pl.pallas_call(
        combine_kernel,
        out_shape=jax.ShapeDtypeStruct((1, NH * GH * HD), BF),
        in_specs=[VMEM],
        out_specs=VMEM,
        compiler_params=params(),
        name="combine",
    )(back.reshape(NB * NH, WIDE))
    return context, parent


def solution(mesh):
    fine = Mesh(mesh.devices.reshape(NX, NZ, NY, NL, NC), ("xh", "z", "y", "xl", "c"))
    blk, head = ("xh", "z", "y"), ("xl", "c")
    both = P(blk, head)
    return jax.shard_map(
        on_device,
        mesh=fine,
        in_specs=(both,) * 6 + (P(), P(), P()),
        out_specs=(both, P(blk + head, None)),
        check_vma=False,
    )
```

```python
import functools
import math

import jax
import jax.numpy as jnp
from jax import lax
from jax.experimental import pallas as pl
from jax.experimental.pallas import tpu as pltpu
from jax.sharding import Mesh
from jax.sharding import PartitionSpec as P

HD = 128
NX, NZ, NY, NL, NC = 2, 8, 4, 2, 2
NB = NX * NZ
NA = NX * NY
NH = NL * NC
GROUPS = 2
PER = 8
GH = GROUPS * PER
TOK = 128
ANC = 16
QR = 4
KVR = TOK + ANC
KEYS = NA * KVR
STRIDE = 4 * ANC
CHUNK = STRIDE + QR * PER
ROWS = NB * QR
LOG2E = 1.4426950408889634
WIDE = PER * HD + 2 * HD
SCALE = LOG2E / math.sqrt(HD)
BF = jnp.bfloat16
F32 = jnp.float32
VMEM = pl.BlockSpec()
SMEM = pl.BlockSpec(memory_space=pltpu.SMEM)


def params(mib=40):
    return pltpu.CompilerParams(vmem_limit_bytes=mib * 1024 * 1024)


def nt(a, b):
    return lax.dot_general(a, b, (((1,), (1,)), ((), ())), preferred_element_type=F32)


def half_kernel(mine, ak, av, pq, ck, cv, out, scr):
    q = pq[...].astype(F32)
    for g in range(GROUPS):
        for r in range(QR):
            for h in range(PER):
                col = (g * PER + h) * HD
                row = (g * QR + r) * PER + h
                scr[row : row + 1, :] = q[r : r + 1, col : col + HD]
    low = lax.axis_index("xh") == (0 if mine else 1)
    at = 0
    for ctx, anc in ((ck, ak), (cv, av)):
        for src in (ctx, anc):
            out[at : at + src.shape[0], :] = jnp.where(low, src[:, :HD], src[:, HD:])
            at = at + src.shape[0]
    for part in (ak[:, :HD], ak[:, HD:], av[:, :HD], av[:, HD:]):
        out[at : at + ANC, :] = part
        at = at + ANC
    q = jnp.where(low, scr[: QR * PER, :], scr[QR * PER :, :])
    out[at:, :] = q.astype(BF)


def send_kernel(own, other, send, kv):
    first = lax.axis_index("xh") == 0
    a, b = own[2 * KVR :, :], other[2 * KVR :, :]
    chunk = jnp.concatenate([jnp.where(first, a, b), jnp.where(first, b, a)], 0)
    for z in range(NZ):
        send[z] = chunk
    for i in range(2):
        kv[0, i] = own[i * KVR : (i + 1) * KVR, :]
        kv[1, i] = other[i * KVR : (i + 1) * KVR, :]


def parent_kernel(bos, qp, got, kv0, kv1, kv2, kv3, out, keys, vals, qpos, turned):
    x, z, y = lax.axis_index("xh"), lax.axis_index("z"), lax.axis_index("y")
    masks = []
    for b in range(NB):
        for r in range(QR):
            row = (b * QR + r) * PER
            at = ((b % NX * NZ + b // NX) * NY + y) * QR + r
            qpos[row : row + PER, :] = jnp.full((PER, HD), qp[at], jnp.int32)
    rows = ROWS * PER
    lane = lax.broadcasted_iota(jnp.int32, (rows, HD), 1)
    for i, kv in enumerate((kv0, kv1, kv2, kv3)):
        for k in range(NX):
            at = i * NX + k
            keys[at * TOK : (at + 1) * TOK, :] = kv[k, 0, :TOK, :]
            vals[at * TOK : (at + 1) * TOK, :] = kv[k, 1, :TOK, :]
            owner = x if k == 0 else 1 - x
            base = bos[(owner * NZ + z) * NY + lax.rem(y + NY - i, NY)] * TOK
            masks.append(lane + base < qpos[...])
            at = NA * TOK + at * ANC
            keys[at : at + ANC, :] = kv[k, 0, TOK:, :]
            vals[at : at + ANC, :] = kv[k, 1, TOK:, :]
    q = got[:, STRIDE:, :].reshape(rows, HD)
    s = nt(q, keys[...]) * SCALE
    s = [s[:, i * HD : (i + 1) * HD] for i in range(KEYS // HD)]
    s = [jnp.where(v, t, -1e30) for v, t in zip(masks, s)] + s[NA:]
    m = jnp.max(functools.reduce(jnp.maximum, s), axis=1, keepdims=True)
    p = [jnp.exp2(v - m) for v in s]
    total = jnp.sum(sum(p[1:], p[0]), axis=1, keepdims=True)
    p = jnp.concatenate([v.astype(BF) for v in p], 1)
    o = jnp.dot(p, vals[...], preferred_element_type=F32)
    turned[0] = o * (1.0 / total)
    turned[1] = jnp.broadcast_to(m + jnp.log2(total), (rows, HD))
    stats = jnp.zeros((ROWS, HD), F32)
    lanes = lax.broadcasted_iota(jnp.int32, (ROWS, HD), 1)
    for h in range(PER):
        pick = pl.ds(h, ROWS, stride=PER)
        out[:, h * HD : (h + 1) * HD] = turned[0, pick, :].astype(BF)
        stats = jnp.where(lanes == h, turned[1, pick, :], stats)
    hi = stats.astype(BF).astype(F32)
    mid = (stats - hi).astype(BF).astype(F32)
    low = stats - hi - mid
    stats = hi + pltpu.roll(mid, PER, 1) + pltpu.roll(low, 2 * PER, 1)
    out[:, PER * HD : PER * HD + HD] = stats.astype(BF)
    out[:, PER * HD + HD :] = jnp.zeros((ROWS, HD), BF)


def context_kernel(bos, lens, q_ref, ck, cv, a0, a1, a2, a3, out, keys, vals):
    slot = (lax.axis_index("xh") * NZ + lax.axis_index("z")) * NY + lax.axis_index("y")
    base = bos[slot] * TOK
    count = NB * ANC
    for i, a in enumerate((a0, a1, a2, a3)):
        for g in range(GROUPS):
            k, v = g * ANC, (GROUPS + g) * ANC
            keys[g, i * count : (i + 1) * count, :] = a[:, k : k + ANC, :].reshape(count, HD)
            vals[g, i * count : (i + 1) * count, :] = a[:, v : v + ANC, :].reshape(count, HD)
    mine = lax.broadcasted_iota(jnp.int32, (TOK, TOK), 0)
    other = lax.broadcasted_iota(jnp.int32, (TOK, TOK), 1)
    visible = other <= mine
    end = jnp.int32(0)
    for j in range(lens.shape[0]):
        end = end + lens[j]
        visible = visible & ((mine + base >= end) == (other + base >= end))
    for g in range(GROUPS):
        own_k = ck[:, g * HD : (g + 1) * HD]
        own_v = cv[:, g * HD : (g + 1) * HD]
        for half in range(4):
            hs = [g * PER + half * 2 + j for j in range(2)]
            q = jnp.concatenate([q_ref[:, h * HD : (h + 1) * HD] for h in hs], 0)
            sa = nt(q, keys[g]) * SCALE
            so = nt(q, own_k) * SCALE
            so = jnp.where(visible[None], so.reshape(2, TOK, TOK), -1e30).reshape(2 * TOK, TOK)
            m = jnp.maximum(jnp.max(sa, axis=1, keepdims=True), jnp.max(so, axis=1, keepdims=True))
            pa = jnp.exp2(sa - m)
            po = jnp.exp2(so - m)
            total = jnp.sum(pa, axis=1, keepdims=True) + jnp.sum(po, axis=1, keepdims=True)
            o = jnp.dot(pa.astype(BF), vals[g], preferred_element_type=F32)
            o = o + jnp.dot(po.astype(BF), own_v, preferred_element_type=F32)
            o = (o / total).astype(BF)
            for j, h in enumerate(hs):
                out[:, h * HD : (h + 1) * HD] = o[j * TOK : (j + 1) * TOK]


def combine_kernel(got, out):
    st = got[:, PER * HD : PER * HD + HD].astype(F32)
    lse = st + pltpu.roll(st, HD - PER, 1) + pltpu.roll(st, HD - 2 * PER, 1)
    lse = lse.reshape(NZ, GROUPS * NH, HD)
    w = jnp.exp2(lse - jnp.max(lse, axis=0, keepdims=True))
    w = (w / jnp.sum(w, axis=0, keepdims=True)).reshape(NZ * GROUPS * NH, HD)
    for h in range(PER):
        x = got[:, h * HD : (h + 1) * HD].astype(F32) * w[:, h : h + 1]
        x = jnp.sum(x.reshape(NZ, GROUPS * NH, HD), axis=0)
        for g in range(GROUPS):
            for k in range(NH):
                at = (k * GH + g * PER + h) * HD
                out[:, at : at + HD] = x[g * NH + k : g * NH + k + 1].astype(BF)


def on_device(cq, ck, cv, ak, av, pq, bos, lens, qp):
    half = jax.ShapeDtypeStruct((2 * KVR + CHUNK, HD), BF)
    own, give = [
        pl.pallas_call(
            functools.partial(half_kernel, mine),
            out_shape=half,
            in_specs=[VMEM] * 5,
            out_specs=VMEM,
            scratch_shapes=[pltpu.VMEM((GROUPS * QR * PER, HD), F32)],
            compiler_params=params(40 if mine else 60),
            cost_estimate=pl.CostEstimate(
                flops=3 * 10**9, bytes_accessed=10**6, transcendentals=0
            ),
            name="own" if mine else "give",
        )(ak, av, pq, ck, cv)
        for mine in (True, False)
    ]
    other = lax.ppermute(give, "xh", [(0, 1), (1, 0)])
    send, kv = pl.pallas_call(
        send_kernel,
        out_shape=(
            jax.ShapeDtypeStruct((NZ, NX * CHUNK, HD), BF),
            jax.ShapeDtypeStruct((NX, 2, KVR, HD), BF),
        ),
        in_specs=[VMEM] * 2,
        out_specs=(VMEM,) * 2,
        compiler_params=params(),
        name="send",
    )(own, other)

    def turn(x, shift):
        return lax.ppermute(x, "y", [(i, (i + shift) % NY) for i in range(NY)])

    kvs = [kv] + [turn(kv, s) for s in (1, 2, 3)]
    got = lax.all_to_all(send, "z", 0, 0, tiled=True).reshape(NB, CHUNK, HD)
    got, *kvs = lax.optimization_barrier((got, *kvs))
    anchors = got[:, :STRIDE]
    anchors = [anchors] + [turn(anchors, s) for s in (1, 2, 3)]
    part = pl.pallas_call(
        parent_kernel,
        out_shape=jax.ShapeDtypeStruct((ROWS, WIDE), BF),
        in_specs=[SMEM] * 2 + [VMEM] * 5,
        out_specs=VMEM,
        scratch_shapes=[
            pltpu.VMEM((KEYS, HD), BF),
            pltpu.VMEM((KEYS, HD), BF),
            pltpu.VMEM((ROWS * PER, HD), jnp.int32),
            pltpu.VMEM((2, ROWS * PER, HD), F32),
        ],
        compiler_params=params(),
        cost_estimate=pl.CostEstimate(flops=10**9, bytes_accessed=2 * 10**6, transcendentals=10**6),
        name="parent",
    )(bos, qp, got, *kvs)
    part = part.reshape(ROWS, 2, WIDE // 2)
    back = lax.all_to_all(part, ("z", "xh", "xl", "c"), 0, 0, tiled=True)
    context = pl.pallas_call(
        context_kernel,
        out_shape=jax.ShapeDtypeStruct((TOK, GH * HD), BF),
        in_specs=[SMEM] * 2 + [VMEM] * 7,
        out_specs=VMEM,
        scratch_shapes=[
            pltpu.VMEM((GROUPS, NY * NB * ANC, HD), BF),
            pltpu.VMEM((GROUPS, NY * NB * ANC, HD), BF),
        ],
        compiler_params=params(),
        cost_estimate=pl.CostEstimate(flops=60 * 10**9, bytes_accessed=4 * 10**6, transcendentals=3 * 10**6),
        name="context",
    )(bos, lens, cq, ck, cv, *anchors)
    parent = pl.pallas_call(
        combine_kernel,
        out_shape=jax.ShapeDtypeStruct((1, NH * GH * HD), BF),
        in_specs=[VMEM],
        out_specs=VMEM,
        compiler_params=params(),
        name="combine",
    )(back.reshape(NB * NH, WIDE))
    return context, parent


def solution(mesh):
    fine = Mesh(mesh.devices.reshape(NX, NZ, NY, NL, NC), ("xh", "z", "y", "xl", "c"))
    blk, head = ("xh", "z", "y"), ("xl", "c")
    both = P(blk, head)
    return jax.shard_map(
        on_device,
        mesh=fine,
        in_specs=(both,) * 6 + (P(), P(), P()),
        out_specs=(both, P(blk + head, None)),
        check_vma=False,
    )
```

```python
import functools
import math

import jax
import jax.numpy as jnp
from jax import lax
from jax.experimental import pallas as pl
from jax.experimental.pallas import tpu as pltpu
from jax.sharding import Mesh
from jax.sharding import PartitionSpec as P

HD = 128
NX, NZ, NY, NL, NC = 2, 8, 4, 2, 2
NB = NX * NZ
NA = NX * NY
NH = NL * NC
GROUPS = 2
PER = 8
GH = GROUPS * PER
TOK = 128
ANC = 16
QR = 4
KVR = TOK + ANC
KEYS = NA * KVR
STRIDE = 4 * ANC
CHUNK = STRIDE + QR * PER
ROWS = NB * QR
SPLIT = 2
LOG2E = 1.4426950408889634
WIDE = PER * HD + 2 * HD
SCALE = LOG2E / math.sqrt(HD)
BF = jnp.bfloat16
F32 = jnp.float32
VMEM = pl.BlockSpec()
SMEM = pl.BlockSpec(memory_space=pltpu.SMEM)


def params(mib=40):
    return pltpu.CompilerParams(vmem_limit_bytes=mib * 1024 * 1024)


def nt(a, b):
    return lax.dot_general(a, b, (((1,), (1,)), ((), ())), preferred_element_type=F32)


def half_kernel(mine, ak, av, pq, ck, cv, out, scr):
    q = pq[...].astype(F32)
    for g in range(GROUPS):
        for r in range(QR):
            for h in range(PER):
                col = (g * PER + h) * HD
                row = (g * QR + r) * PER + h
                scr[row : row + 1, :] = q[r : r + 1, col : col + HD]
    low = lax.axis_index("xh") == (0 if mine else 1)
    at = 0
    for ctx, anc in ((ck, ak), (cv, av)):
        for src in (ctx, anc):
            out[at : at + src.shape[0], :] = jnp.where(low, src[:, :HD], src[:, HD:])
            at = at + src.shape[0]
    for part in (ak[:, :HD], ak[:, HD:], av[:, :HD], av[:, HD:]):
        out[at : at + ANC, :] = part
        at = at + ANC
    q = jnp.where(low, scr[: QR * PER, :], scr[QR * PER :, :])
    out[at:, :] = q.astype(BF)


def send_kernel(own, other, send, kv):
    first = lax.axis_index("xh") == 0
    a, b = own[2 * KVR :, :], other[2 * KVR :, :]
    chunk = jnp.concatenate([jnp.where(first, a, b), jnp.where(first, b, a)], 0)
    for z in range(NZ):
        send[z] = chunk
    for i in range(2):
        kv[0, i] = own[i * KVR : (i + 1) * KVR, :]
        kv[1, i] = other[i * KVR : (i + 1) * KVR, :]


def parent_kernel(bos, qp, got, kv0, kv1, kv2, kv3, out, keys, vals, qpos, turned):
    x, z, y = lax.axis_index("xh"), lax.axis_index("z"), lax.axis_index("y")
    for b in range(NB):
        for r in range(QR):
            row = (b * QR + r) * PER
            at = ((b % NX * NZ + b // NX) * NY + y) * QR + r
            qpos[row : row + PER, :] = jnp.full((PER, HD), qp[at], jnp.int32)
    bases = []
    for i, kv in enumerate((kv0, kv1, kv2, kv3)):
        for k in range(NX):
            at = i * NX + k
            keys[at * TOK : (at + 1) * TOK, :] = kv[k, 0, :TOK, :]
            vals[at * TOK : (at + 1) * TOK, :] = kv[k, 1, :TOK, :]
            owner = x if k == 0 else 1 - x
            bases.append(bos[(owner * NZ + z) * NY + lax.bitwise_xor(y, jnp.int32(i))] * TOK)
            at = NA * TOK + at * ANC
            keys[at : at + ANC, :] = kv[k, 0, TOK:, :]
            vals[at : at + ANC, :] = kv[k, 1, TOK:, :]
    rows = ROWS * PER // SPLIT
    lane = lax.broadcasted_iota(jnp.int32, (rows, HD), 1)
    for t in range(SPLIT):
        mine = slice(t * rows, (t + 1) * rows)
        reach = qpos[mine, :] - lane
        q = got[t * NB // SPLIT : (t + 1) * NB // SPLIT, STRIDE:, :].reshape(rows, HD)
        s = nt(q, keys[...])
        s = [s[:, i * HD : (i + 1) * HD] for i in range(KEYS // HD)]
        s = [jnp.where(v < reach, u, -1e30) for v, u in zip(bases, s)] + s[NA:]
        m = jnp.max(functools.reduce(jnp.maximum, s), axis=1, keepdims=True)
        p = [jnp.exp2((v - m) * SCALE) for v in s]
        total = jnp.sum(sum(p[1:], p[0]), axis=1, keepdims=True)
        p = jnp.concatenate([v.astype(BF) for v in p], 1)
        o = jnp.dot(p, vals[...], preferred_element_type=F32)
        turned[0, mine, :] = o * (1.0 / total)
        turned[1, mine, :] = jnp.broadcast_to(m * SCALE + jnp.log2(total), (rows, HD))
    stats = jnp.zeros((ROWS, HD), F32)
    lanes = lax.broadcasted_iota(jnp.int32, (ROWS, HD), 1)
    for h in range(PER):
        pick = pl.ds(h, ROWS, stride=PER)
        out[:, h * HD : (h + 1) * HD] = turned[0, pick, :].astype(BF)
        stats = jnp.where(lanes == h, turned[1, pick, :], stats)
    hi = stats.astype(BF).astype(F32)
    mid = (stats - hi).astype(BF).astype(F32)
    low = stats - hi - mid
    stats = hi + pltpu.roll(mid, PER, 1) + pltpu.roll(low, 2 * PER, 1)
    out[:, PER * HD : PER * HD + HD] = stats.astype(BF)
    out[:, PER * HD + HD :] = jnp.zeros((ROWS, HD), BF)


def context_kernel(bos, lens, q_ref, ck, cv, a0, a1, a2, a3, out, keys, vals):
    slot = (lax.axis_index("xh") * NZ + lax.axis_index("z")) * NY + lax.axis_index("y")
    base = bos[slot] * TOK
    count = NB * ANC
    for i, a in enumerate((a0, a1, a2, a3)):
        for g in range(GROUPS):
            k, v = g * ANC, (GROUPS + g) * ANC
            keys[g, i * count : (i + 1) * count, :] = a[:, k : k + ANC, :].reshape(count, HD)
            vals[g, i * count : (i + 1) * count, :] = a[:, v : v + ANC, :].reshape(count, HD)
    mine = lax.broadcasted_iota(jnp.int32, (TOK, TOK), 0)
    other = lax.broadcasted_iota(jnp.int32, (TOK, TOK), 1)
    visible = other <= mine
    end = jnp.int32(0)
    for j in range(lens.shape[0]):
        end = end + lens[j]
        visible = visible & ((mine + base >= end) == (other + base >= end))
    for g in range(GROUPS):
        own_k = ck[:, g * HD : (g + 1) * HD]
        own_v = cv[:, g * HD : (g + 1) * HD]
        for half in range(4):
            hs = [g * PER + half * 2 + j for j in range(2)]
            q = jnp.concatenate([q_ref[:, h * HD : (h + 1) * HD] for h in hs], 0)
            sa = nt(q, keys[g]) * SCALE
            so = nt(q, own_k) * SCALE
            so = jnp.where(visible[None], so.reshape(2, TOK, TOK), -1e30).reshape(2 * TOK, TOK)
            m = jnp.maximum(jnp.max(sa, axis=1, keepdims=True), jnp.max(so, axis=1, keepdims=True))
            pa = jnp.exp2(sa - m)
            po = jnp.exp2(so - m)
            total = jnp.sum(pa, axis=1, keepdims=True) + jnp.sum(po, axis=1, keepdims=True)
            o = jnp.dot(pa.astype(BF), vals[g], preferred_element_type=F32)
            o = o + jnp.dot(po.astype(BF), own_v, preferred_element_type=F32)
            o = (o / total).astype(BF)
            for j, h in enumerate(hs):
                out[:, h * HD : (h + 1) * HD] = o[j * TOK : (j + 1) * TOK]


def combine_kernel(got, out):
    st = got[:, PER * HD : PER * HD + HD].astype(F32)
    lse = st + pltpu.roll(st, HD - PER, 1) + pltpu.roll(st, HD - 2 * PER, 1)
    lse = lse.reshape(NZ, GROUPS * NH, HD)
    w = jnp.exp2(lse - jnp.max(lse, axis=0, keepdims=True))
    w = (w / jnp.sum(w, axis=0, keepdims=True)).reshape(NZ * GROUPS * NH, HD)
    for h in range(PER):
        x = got[:, h * HD : (h + 1) * HD].astype(F32) * w[:, h : h + 1]
        x = jnp.sum(x.reshape(NZ, GROUPS * NH, HD), axis=0)
        for g in range(GROUPS):
            for k in range(NH):
                at = (k * GH + g * PER + h) * HD
                out[:, at : at + HD] = x[g * NH + k : g * NH + k + 1].astype(BF)


def on_device(cq, ck, cv, ak, av, pq, bos, lens, qp):
    half = jax.ShapeDtypeStruct((2 * KVR + CHUNK, HD), BF)
    own, give = [
        pl.pallas_call(
            functools.partial(half_kernel, mine),
            out_shape=half,
            in_specs=[VMEM] * 5,
            out_specs=VMEM,
            scratch_shapes=[pltpu.VMEM((GROUPS * QR * PER, HD), F32)],
            compiler_params=params(40 if mine else 60),
            cost_estimate=pl.CostEstimate(
                flops=3 * 10**9, bytes_accessed=10**6, transcendentals=0
            ),
            name="own" if mine else "give",
        )(ak, av, pq, ck, cv)
        for mine in (True, False)
    ]
    other = lax.ppermute(give, "xh", [(0, 1), (1, 0)])
    send, kv = pl.pallas_call(
        send_kernel,
        out_shape=(
            jax.ShapeDtypeStruct((NZ, NX * CHUNK, HD), BF),
            jax.ShapeDtypeStruct((NX, 2, KVR, HD), BF),
        ),
        in_specs=[VMEM] * 2,
        out_specs=(VMEM,) * 2,
        compiler_params=params(),
        name="send",
    )(own, other)

    def turn(x, shift):
        return lax.ppermute(x, "y", [(i, i ^ shift) for i in range(NY)])

    kvs = [kv] + [turn(kv, s) for s in (1, 2, 3)]
    got = lax.all_to_all(send, "z", 0, 0, tiled=True).reshape(NB, CHUNK, HD)
    got, *kvs = lax.optimization_barrier((got, *kvs))
    anchors = got[:, :STRIDE]
    anchors = [anchors] + [turn(anchors, s) for s in (1, 2, 3)]
    part = pl.pallas_call(
        parent_kernel,
        out_shape=jax.ShapeDtypeStruct((ROWS, WIDE), BF),
        in_specs=[SMEM] * 2 + [VMEM] * 5,
        out_specs=VMEM,
        scratch_shapes=[
            pltpu.VMEM((KEYS, HD), BF),
            pltpu.VMEM((KEYS, HD), BF),
            pltpu.VMEM((ROWS * PER, HD), jnp.int32),
            pltpu.VMEM((2, ROWS * PER, HD), F32),
        ],
        compiler_params=params(),
        cost_estimate=pl.CostEstimate(flops=10**9, bytes_accessed=2 * 10**6, transcendentals=10**6),
        name="parent",
    )(bos, qp, got, *kvs)
    part = part.reshape(ROWS, 2, WIDE // 2)
    back = lax.all_to_all(part, ("z", "xh", "xl", "c"), 0, 0, tiled=True)
    context = pl.pallas_call(
        context_kernel,
        out_shape=jax.ShapeDtypeStruct((TOK, GH * HD), BF),
        in_specs=[SMEM] * 2 + [VMEM] * 7,
        out_specs=VMEM,
        scratch_shapes=[
            pltpu.VMEM((GROUPS, NY * NB * ANC, HD), BF),
            pltpu.VMEM((GROUPS, NY * NB * ANC, HD), BF),
        ],
        compiler_params=params(),
        cost_estimate=pl.CostEstimate(flops=60 * 10**9, bytes_accessed=4 * 10**6, transcendentals=3 * 10**6),
        name="context",
    )(bos, lens, cq, ck, cv, *anchors)
    parent = pl.pallas_call(
        combine_kernel,
        out_shape=jax.ShapeDtypeStruct((1, NH * GH * HD), BF),
        in_specs=[VMEM],
        out_specs=VMEM,
        compiler_params=params(),
        name="combine",
    )(back.reshape(NB * NH, WIDE))
    return context, parent


def solution(mesh):
    fine = Mesh(mesh.devices.reshape(NX, NZ, NY, NL, NC), ("xh", "z", "y", "xl", "c"))
    blk, head = ("xh", "z", "y"), ("xl", "c")
    both = P(blk, head)
    return jax.shard_map(
        on_device,
        mesh=fine,
        in_specs=(both,) * 6 + (P(), P(), P()),
        out_specs=(both, P(blk + head, None)),
        check_vma=False,
    )
```

```python
import functools
import math

import jax
import jax.numpy as jnp
from jax import lax
from jax.experimental import pallas as pl
from jax.experimental.pallas import tpu as pltpu
from jax.sharding import Mesh
from jax.sharding import PartitionSpec as P

HD = 128
NX, NZ, NY, NL, NC = 2, 8, 4, 2, 2
NB = NX * NZ
NA = NX * NY
NH = NL * NC
GROUPS = 2
PER = 8
GH = GROUPS * PER
TOK = 128
ANC = 16
QR = 4
KVR = TOK + ANC
KEYS = NA * KVR
STRIDE = 4 * ANC
CHUNK = STRIDE + QR * PER
ROWS = NB * QR
SPLIT = 2
LOG2E = 1.4426950408889634
WIDE = PER * HD + 2 * HD
SCALE = LOG2E / math.sqrt(HD)
BF = jnp.bfloat16
F32 = jnp.float32
VMEM = pl.BlockSpec()
SMEM = pl.BlockSpec(memory_space=pltpu.SMEM)


def params(mib=40):
    return pltpu.CompilerParams(vmem_limit_bytes=mib * 1024 * 1024)


def nt(a, b):
    return lax.dot_general(a, b, (((1,), (1,)), ((), ())), preferred_element_type=F32)


def half_kernel(mine, ak, av, pq, ck, cv, out, scr):
    low = lax.axis_index("xh") == (0 if mine else 1)
    q = jnp.where(low, pq[:, : PER * HD], pq[:, PER * HD :]).astype(F32)
    for r in range(QR):
        for h in range(PER):
            row = r * PER + h
            scr[row : row + 1, :] = q[r : r + 1, h * HD : (h + 1) * HD]
    at = 0
    for ctx, anc in ((ck, ak), (cv, av)):
        for src in (ctx, anc):
            out[at : at + src.shape[0], :] = jnp.where(low, src[:, :HD], src[:, HD:])
            at = at + src.shape[0]
    for part in (ak[:, :HD], ak[:, HD:], av[:, :HD], av[:, HD:]):
        out[at : at + ANC, :] = part
        at = at + ANC
    out[at:, :] = scr[...].astype(BF)


def send_kernel(own, other, send, kv):
    first = lax.axis_index("xh") == 0
    a, b = own[2 * KVR :, :], other[2 * KVR :, :]
    chunk = jnp.concatenate([jnp.where(first, a, b), jnp.where(first, b, a)], 0)
    for z in range(NZ):
        send[z] = chunk
    for i in range(2):
        kv[0, i] = own[i * KVR : (i + 1) * KVR, :]
        kv[1, i] = other[i * KVR : (i + 1) * KVR, :]


def parent_kernel(bos, qp, got, kv0, kv1, kv2, kv3, out, keys, vals, qpos, turned):
    x, z, y = lax.axis_index("xh"), lax.axis_index("z"), lax.axis_index("y")
    for b in range(NB):
        for r in range(QR):
            row = (b * QR + r) * PER
            at = ((b % NX * NZ + b // NX) * NY + y) * QR + r
            qpos[row : row + PER, :] = jnp.full((PER, HD), qp[at], jnp.int32)
    bases = []
    for i, kv in enumerate((kv0, kv1, kv2, kv3)):
        for k in range(NX):
            at = i * NX + k
            keys[at * TOK : (at + 1) * TOK, :] = kv[k, 0, :TOK, :]
            vals[at * TOK : (at + 1) * TOK, :] = kv[k, 1, :TOK, :]
            owner = x if k == 0 else 1 - x
            bases.append(bos[(owner * NZ + z) * NY + lax.bitwise_xor(y, jnp.int32(i))] * TOK)
            at = NA * TOK + at * ANC
            keys[at : at + ANC, :] = kv[k, 0, TOK:, :]
            vals[at : at + ANC, :] = kv[k, 1, TOK:, :]
    rows = ROWS * PER // SPLIT
    lane = lax.broadcasted_iota(jnp.int32, (rows, HD), 1)
    for t in range(SPLIT):
        mine = slice(t * rows, (t + 1) * rows)
        reach = qpos[mine, :] - lane
        q = got[t * NB // SPLIT : (t + 1) * NB // SPLIT, STRIDE:, :].reshape(rows, HD)
        s = nt(q, keys[...])
        s = [s[:, i * HD : (i + 1) * HD] for i in range(KEYS // HD)]
        s = [jnp.where(v < reach, u, -1e30) for v, u in zip(bases, s)] + s[NA:]
        m = jnp.max(functools.reduce(jnp.maximum, s), axis=1, keepdims=True)
        p = [jnp.exp2((v - m) * SCALE) for v in s]
        total = jnp.sum(sum(p[1:], p[0]), axis=1, keepdims=True)
        p = jnp.concatenate([v.astype(BF) for v in p], 1)
        o = jnp.dot(p, vals[...], preferred_element_type=F32)
        turned[0, mine, :] = o * (1.0 / total)
        turned[1, mine, :] = jnp.broadcast_to(m * SCALE + jnp.log2(total), (rows, HD))
    stats = jnp.zeros((ROWS, HD), F32)
    lanes = lax.broadcasted_iota(jnp.int32, (ROWS, HD), 1)
    for h in range(PER):
        pick = pl.ds(h, ROWS, stride=PER)
        out[:, h * HD : (h + 1) * HD] = turned[0, pick, :].astype(BF)
        stats = jnp.where(lanes == h, turned[1, pick, :], stats)
    hi = stats.astype(BF).astype(F32)
    mid = (stats - hi).astype(BF).astype(F32)
    low = stats - hi - mid
    stats = hi + pltpu.roll(mid, PER, 1) + pltpu.roll(low, 2 * PER, 1)
    out[:, PER * HD : PER * HD + HD] = stats.astype(BF)
    out[:, PER * HD + HD :] = jnp.zeros((ROWS, HD), BF)


def context_kernel(bos, lens, q_ref, ck, cv, a0, a1, a2, a3, out, keys, vals):
    slot = (lax.axis_index("xh") * NZ + lax.axis_index("z")) * NY + lax.axis_index("y")
    base = bos[slot] * TOK
    count = NB * ANC
    for i, a in enumerate((a0, a1, a2, a3)):
        for g in range(GROUPS):
            k, v = g * ANC, (GROUPS + g) * ANC
            keys[g, i * count : (i + 1) * count, :] = a[:, k : k + ANC, :].reshape(count, HD)
            vals[g, i * count : (i + 1) * count, :] = a[:, v : v + ANC, :].reshape(count, HD)
    mine = lax.broadcasted_iota(jnp.int32, (TOK, TOK), 0)
    other = lax.broadcasted_iota(jnp.int32, (TOK, TOK), 1)
    visible = other <= mine
    end = jnp.int32(0)
    for j in range(lens.shape[0]):
        end = end + lens[j]
        visible = visible & ((mine + base >= end) == (other + base >= end))
    for g in range(GROUPS):
        own_k = ck[:, g * HD : (g + 1) * HD]
        own_v = cv[:, g * HD : (g + 1) * HD]
        for half in range(4):
            hs = [g * PER + half * 2 + j for j in range(2)]
            q = jnp.concatenate([q_ref[:, h * HD : (h + 1) * HD] for h in hs], 0)
            sa = nt(q, keys[g]) * SCALE
            so = nt(q, own_k) * SCALE
            so = jnp.where(visible[None], so.reshape(2, TOK, TOK), -1e30).reshape(2 * TOK, TOK)
            m = jnp.maximum(jnp.max(sa, axis=1, keepdims=True), jnp.max(so, axis=1, keepdims=True))
            pa = jnp.exp2(sa - m)
            po = jnp.exp2(so - m)
            total = jnp.sum(pa, axis=1, keepdims=True) + jnp.sum(po, axis=1, keepdims=True)
            o = jnp.dot(pa.astype(BF), vals[g], preferred_element_type=F32)
            o = o + jnp.dot(po.astype(BF), own_v, preferred_element_type=F32)
            o = (o / total).astype(BF)
            for j, h in enumerate(hs):
                out[:, h * HD : (h + 1) * HD] = o[j * TOK : (j + 1) * TOK]


def combine_kernel(got, out):
    st = got[:, PER * HD : PER * HD + HD].astype(F32)
    lse = st + pltpu.roll(st, HD - PER, 1) + pltpu.roll(st, HD - 2 * PER, 1)
    lse = lse.reshape(NZ, GROUPS * NH, HD)
    w = jnp.exp2(lse - jnp.max(lse, axis=0, keepdims=True))
    w = (w / jnp.sum(w, axis=0, keepdims=True)).reshape(NZ * GROUPS * NH, HD)
    for h in range(PER):
        x = got[:, h * HD : (h + 1) * HD].astype(F32) * w[:, h : h + 1]
        x = jnp.sum(x.reshape(NZ, GROUPS * NH, HD), axis=0)
        for g in range(GROUPS):
            for k in range(NH):
                at = (k * GH + g * PER + h) * HD
                out[:, at : at + HD] = x[g * NH + k : g * NH + k + 1].astype(BF)


def on_device(cq, ck, cv, ak, av, pq, bos, lens, qp):
    half = jax.ShapeDtypeStruct((2 * KVR + CHUNK, HD), BF)
    own, give = [
        pl.pallas_call(
            functools.partial(half_kernel, mine),
            out_shape=half,
            in_specs=[VMEM] * 5,
            out_specs=VMEM,
            scratch_shapes=[pltpu.VMEM((QR * PER, HD), F32)],
            compiler_params=params(40 if mine else 60),
            cost_estimate=pl.CostEstimate(
                flops=3 * 10**9, bytes_accessed=10**6, transcendentals=0
            ),
            name="own" if mine else "give",
        )(ak, av, pq, ck, cv)
        for mine in (True, False)
    ]
    other = lax.ppermute(give, "xh", [(0, 1), (1, 0)])
    send, kv = pl.pallas_call(
        send_kernel,
        out_shape=(
            jax.ShapeDtypeStruct((NZ, NX * CHUNK, HD), BF),
            jax.ShapeDtypeStruct((NX, 2, KVR, HD), BF),
        ),
        in_specs=[VMEM] * 2,
        out_specs=(VMEM,) * 2,
        compiler_params=params(),
        name="send",
    )(own, other)

    def turn(x, shift):
        return lax.ppermute(x, "y", [(i, i ^ shift) for i in range(NY)])

    kvs = [kv] + [turn(kv, s) for s in (1, 2, 3)]
    got = lax.all_to_all(send, "z", 0, 0, tiled=True).reshape(NB, CHUNK, HD)
    got, *kvs = lax.optimization_barrier((got, *kvs))
    anchors = got[:, :STRIDE]
    anchors = [anchors] + [turn(anchors, s) for s in (1, 2, 3)]
    part = pl.pallas_call(
        parent_kernel,
        out_shape=jax.ShapeDtypeStruct((ROWS, WIDE), BF),
        in_specs=[SMEM] * 2 + [VMEM] * 5,
        out_specs=VMEM,
        scratch_shapes=[
            pltpu.VMEM((KEYS, HD), BF),
            pltpu.VMEM((KEYS, HD), BF),
            pltpu.VMEM((ROWS * PER, HD), jnp.int32),
            pltpu.VMEM((2, ROWS * PER, HD), F32),
        ],
        compiler_params=params(),
        cost_estimate=pl.CostEstimate(flops=10**9, bytes_accessed=2 * 10**6, transcendentals=10**6),
        name="parent",
    )(bos, qp, got, *kvs)
    part = part.reshape(ROWS, 2, WIDE // 2)
    back = lax.all_to_all(part, ("z", "xh", "xl", "c"), 0, 0, tiled=True)
    context = pl.pallas_call(
        context_kernel,
        out_shape=jax.ShapeDtypeStruct((TOK, GH * HD), BF),
        in_specs=[SMEM] * 2 + [VMEM] * 7,
        out_specs=VMEM,
        scratch_shapes=[
            pltpu.VMEM((GROUPS, NY * NB * ANC, HD), BF),
            pltpu.VMEM((GROUPS, NY * NB * ANC, HD), BF),
        ],
        compiler_params=params(),
        cost_estimate=pl.CostEstimate(flops=60 * 10**9, bytes_accessed=4 * 10**6, transcendentals=3 * 10**6),
        name="context",
    )(bos, lens, cq, ck, cv, *anchors)
    parent = pl.pallas_call(
        combine_kernel,
        out_shape=jax.ShapeDtypeStruct((1, NH * GH * HD), BF),
        in_specs=[VMEM],
        out_specs=VMEM,
        compiler_params=params(),
        name="combine",
    )(back.reshape(NB * NH, WIDE))
    return context, parent


def solution(mesh):
    fine = Mesh(mesh.devices.reshape(NX, NZ, NY, NL, NC), ("xh", "z", "y", "xl", "c"))
    blk, head = ("xh", "z", "y"), ("xl", "c")
    both = P(blk, head)
    return jax.shard_map(
        on_device,
        mesh=fine,
        in_specs=(both,) * 6 + (P(), P(), P()),
        out_specs=(both, P(blk + head, None)),
        check_vma=False,
    )
```

```python
import functools
import math

import jax
import jax.numpy as jnp
from jax import lax
from jax.experimental import pallas as pl
from jax.experimental.pallas import tpu as pltpu
from jax.sharding import Mesh
from jax.sharding import PartitionSpec as P

HD = 128
NX, NZ, NY, NL, NC = 2, 8, 4, 2, 2
NB = NX * NZ
NA = NX * NY
NH = NL * NC
GROUPS = 2
PER = 8
GH = GROUPS * PER
TOK = 128
ANC = 16
QR = 4
KVR = TOK + ANC
KEYS = NA * KVR
STRIDE = 4 * ANC
CHUNK = STRIDE + QR * PER
ROWS = NB * QR
SPLIT = 2
LOG2E = 1.4426950408889634
WIDE = PER * HD + 2 * HD
SCALE = LOG2E / math.sqrt(HD)
BF = jnp.bfloat16
F32 = jnp.float32
VMEM = pl.BlockSpec()
SMEM = pl.BlockSpec(memory_space=pltpu.SMEM)


def params(mib=40):
    return pltpu.CompilerParams(vmem_limit_bytes=mib * 1024 * 1024)


def nt(a, b):
    return lax.dot_general(a, b, (((1,), (1,)), ((), ())), preferred_element_type=F32)


def half_kernel(mine, ak, av, pq, ck, cv, out, scr):
    low = lax.axis_index("xh") == (0 if mine else 1)
    q = jnp.where(low, pq[:, : PER * HD], pq[:, PER * HD :]).astype(F32)
    for r in range(QR):
        for h in range(PER):
            row = r * PER + h
            scr[row : row + 1, :] = q[r : r + 1, h * HD : (h + 1) * HD]
    at = 0
    for ctx, anc in ((ck, ak), (cv, av)):
        for src in (ctx, anc):
            out[at : at + src.shape[0], :] = jnp.where(low, src[:, :HD], src[:, HD:])
            at = at + src.shape[0]
    for part in (ak[:, :HD], ak[:, HD:], av[:, :HD], av[:, HD:]):
        out[at : at + ANC, :] = part
        at = at + ANC
    out[at:, :] = scr[...].astype(BF)


def send_kernel(own, other, send, kv):
    first = lax.axis_index("xh") == 0
    a, b = own[2 * KVR :, :], other[2 * KVR :, :]
    chunk = jnp.concatenate([jnp.where(first, a, b), jnp.where(first, b, a)], 0)
    for z in range(NZ):
        send[z] = chunk
    for i in range(2):
        kv[0, i] = own[i * KVR : (i + 1) * KVR, :]
        kv[1, i] = other[i * KVR : (i + 1) * KVR, :]


def parent_kernel(bos, qp, got, kv0, kv1, kv2, kv3, out, keys, vals, qpos, turned):
    x, z, y = lax.axis_index("xh"), lax.axis_index("z"), lax.axis_index("y")
    for b in range(NB):
        for r in range(QR):
            row = (b * QR + r) * PER
            at = ((b % NX * NZ + b // NX) * NY + y) * QR + r
            qpos[row : row + PER, :] = jnp.full((PER, HD), qp[at], jnp.int32)
    bases = []
    for i, kv in enumerate((kv0, kv1, kv2, kv3)):
        for k in range(NX):
            at = i * NX + k
            keys[at * TOK : (at + 1) * TOK, :] = kv[k, 0, :TOK, :]
            vals[at * TOK : (at + 1) * TOK, :] = kv[k, 1, :TOK, :]
            owner = x if k == 0 else 1 - x
            bases.append(bos[(owner * NZ + z) * NY + lax.rem(y + NY - i, NY)] * TOK)
            at = NA * TOK + at * ANC
            keys[at : at + ANC, :] = kv[k, 0, TOK:, :]
            vals[at : at + ANC, :] = kv[k, 1, TOK:, :]
    rows = ROWS * PER // SPLIT
    lane = lax.broadcasted_iota(jnp.int32, (rows, HD), 1)
    for t in range(SPLIT):
        mine = slice(t * rows, (t + 1) * rows)
        reach = qpos[mine, :] - lane
        q = got[t * NB // SPLIT : (t + 1) * NB // SPLIT, STRIDE:, :].reshape(rows, HD)
        s = nt(q, keys[...])
        s = [s[:, i * HD : (i + 1) * HD] for i in range(KEYS // HD)]
        s = [jnp.where(v < reach, u, -1e30) for v, u in zip(bases, s)] + s[NA:]
        m = jnp.max(functools.reduce(jnp.maximum, s), axis=1, keepdims=True)
        p = [jnp.exp2((v - m) * SCALE) for v in s]
        total = jnp.sum(sum(p[1:], p[0]), axis=1, keepdims=True)
        p = jnp.concatenate([v.astype(BF) for v in p], 1)
        o = jnp.dot(p, vals[...], preferred_element_type=F32)
        turned[0, mine, :] = o * (1.0 / total)
        turned[1, mine, :] = jnp.broadcast_to(m * SCALE + jnp.log2(total), (rows, HD))
    stats = jnp.zeros((ROWS, HD), F32)
    lanes = lax.broadcasted_iota(jnp.int32, (ROWS, HD), 1)
    for h in range(PER):
        pick = pl.ds(h, ROWS, stride=PER)
        out[:, h * HD : (h + 1) * HD] = turned[0, pick, :].astype(BF)
        stats = jnp.where(lanes == h, turned[1, pick, :], stats)
    hi = stats.astype(BF).astype(F32)
    mid = (stats - hi).astype(BF).astype(F32)
    low = stats - hi - mid
    stats = hi + pltpu.roll(mid, PER, 1) + pltpu.roll(low, 2 * PER, 1)
    out[:, PER * HD : PER * HD + HD] = stats.astype(BF)
    out[:, PER * HD + HD :] = jnp.zeros((ROWS, HD), BF)


def context_kernel(bos, lens, q_ref, ck, cv, a0, a1, a2, a3, out, keys, vals):
    slot = (lax.axis_index("xh") * NZ + lax.axis_index("z")) * NY + lax.axis_index("y")
    base = bos[slot] * TOK
    count = NB * ANC
    for i, a in enumerate((a0, a1, a2, a3)):
        for g in range(GROUPS):
            k, v = g * ANC, (GROUPS + g) * ANC
            keys[g, i * count : (i + 1) * count, :] = a[:, k : k + ANC, :].reshape(count, HD)
            vals[g, i * count : (i + 1) * count, :] = a[:, v : v + ANC, :].reshape(count, HD)
    mine = lax.broadcasted_iota(jnp.int32, (TOK, TOK), 0)
    other = lax.broadcasted_iota(jnp.int32, (TOK, TOK), 1)
    visible = other <= mine
    end = jnp.int32(0)
    for j in range(lens.shape[0]):
        end = end + lens[j]
        visible = visible & ((mine + base >= end) == (other + base >= end))
    for g in range(GROUPS):
        own_k = ck[:, g * HD : (g + 1) * HD]
        own_v = cv[:, g * HD : (g + 1) * HD]
        for half in range(4):
            hs = [g * PER + half * 2 + j for j in range(2)]
            q = jnp.concatenate([q_ref[:, h * HD : (h + 1) * HD] for h in hs], 0)
            sa = nt(q, keys[g]) * SCALE
            so = nt(q, own_k) * SCALE
            so = jnp.where(visible[None], so.reshape(2, TOK, TOK), -1e30).reshape(2 * TOK, TOK)
            m = jnp.maximum(jnp.max(sa, axis=1, keepdims=True), jnp.max(so, axis=1, keepdims=True))
            pa = jnp.exp2(sa - m)
            po = jnp.exp2(so - m)
            total = jnp.sum(pa, axis=1, keepdims=True) + jnp.sum(po, axis=1, keepdims=True)
            o = jnp.dot(pa.astype(BF), vals[g], preferred_element_type=F32)
            o = o + jnp.dot(po.astype(BF), own_v, preferred_element_type=F32)
            o = (o / total).astype(BF)
            for j, h in enumerate(hs):
                out[:, h * HD : (h + 1) * HD] = o[j * TOK : (j + 1) * TOK]


def combine_kernel(got, out):
    st = got[:, PER * HD : PER * HD + HD].astype(F32)
    lse = st + pltpu.roll(st, HD - PER, 1) + pltpu.roll(st, HD - 2 * PER, 1)
    lse = lse.reshape(NZ, GROUPS * NH, HD)
    w = jnp.exp2(lse - jnp.max(lse, axis=0, keepdims=True))
    w = (w / jnp.sum(w, axis=0, keepdims=True)).reshape(NZ * GROUPS * NH, HD)
    for h in range(PER):
        x = got[:, h * HD : (h + 1) * HD].astype(F32) * w[:, h : h + 1]
        x = jnp.sum(x.reshape(NZ, GROUPS * NH, HD), axis=0)
        for g in range(GROUPS):
            for k in range(NH):
                at = (k * GH + g * PER + h) * HD
                out[:, at : at + HD] = x[g * NH + k : g * NH + k + 1].astype(BF)


def on_device(cq, ck, cv, ak, av, pq, bos, lens, qp):
    half = jax.ShapeDtypeStruct((2 * KVR + CHUNK, HD), BF)
    own, give = [
        pl.pallas_call(
            functools.partial(half_kernel, mine),
            out_shape=half,
            in_specs=[VMEM] * 5,
            out_specs=VMEM,
            scratch_shapes=[pltpu.VMEM((QR * PER, HD), F32)],
            compiler_params=params(40 if mine else 60),
            cost_estimate=pl.CostEstimate(
                flops=3 * 10**9, bytes_accessed=10**6, transcendentals=0
            ),
            name="own" if mine else "give",
        )(ak, av, pq, ck, cv)
        for mine in (True, False)
    ]
    other = lax.ppermute(give, "xh", [(0, 1), (1, 0)])
    send, kv = pl.pallas_call(
        send_kernel,
        out_shape=(
            jax.ShapeDtypeStruct((NZ, NX * CHUNK, HD), BF),
            jax.ShapeDtypeStruct((NX, 2, KVR, HD), BF),
        ),
        in_specs=[VMEM] * 2,
        out_specs=(VMEM,) * 2,
        compiler_params=params(),
        name="send",
    )(own, other)

    def turn(x, shift):
        return lax.ppermute(x, "y", [(i, (i + shift) % NY) for i in range(NY)])

    kvs = [kv] + [turn(kv, s) for s in (1, 2, 3)]
    got = lax.all_to_all(send, "z", 0, 0, tiled=True).reshape(NB, CHUNK, HD)
    got, *kvs = lax.optimization_barrier((got, *kvs))
    anchors = got[:, :STRIDE]
    anchors = [anchors] + [turn(anchors, s) for s in (1, 2, 3)]
    part = pl.pallas_call(
        parent_kernel,
        out_shape=jax.ShapeDtypeStruct((ROWS, WIDE), BF),
        in_specs=[SMEM] * 2 + [VMEM] * 5,
        out_specs=VMEM,
        scratch_shapes=[
            pltpu.VMEM((KEYS, HD), BF),
            pltpu.VMEM((KEYS, HD), BF),
            pltpu.VMEM((ROWS * PER, HD), jnp.int32),
            pltpu.VMEM((2, ROWS * PER, HD), F32),
        ],
        compiler_params=params(),
        cost_estimate=pl.CostEstimate(flops=10**9, bytes_accessed=2 * 10**6, transcendentals=10**6),
        name="parent",
    )(bos, qp, got, *kvs)
    part = part.reshape(ROWS, 2, WIDE // 2)
    back = lax.all_to_all(part, ("z", "xh", "xl", "c"), 0, 0, tiled=True)
    context = pl.pallas_call(
        context_kernel,
        out_shape=jax.ShapeDtypeStruct((TOK, GH * HD), BF),
        in_specs=[SMEM] * 2 + [VMEM] * 7,
        out_specs=VMEM,
        scratch_shapes=[
            pltpu.VMEM((GROUPS, NY * NB * ANC, HD), BF),
            pltpu.VMEM((GROUPS, NY * NB * ANC, HD), BF),
        ],
        compiler_params=params(),
        cost_estimate=pl.CostEstimate(flops=60 * 10**9, bytes_accessed=4 * 10**6, transcendentals=3 * 10**6),
        name="context",
    )(bos, lens, cq, ck, cv, *anchors)
    parent = pl.pallas_call(
        combine_kernel,
        out_shape=jax.ShapeDtypeStruct((1, NH * GH * HD), BF),
        in_specs=[VMEM],
        out_specs=VMEM,
        compiler_params=params(),
        name="combine",
    )(back.reshape(NB * NH, WIDE))
    return context, parent


def solution(mesh):
    fine = Mesh(mesh.devices.reshape(NX, NZ, NY, NL, NC), ("xh", "z", "y", "xl", "c"))
    blk, head = ("xh", "z", "y"), ("xl", "c")
    both = P(blk, head)
    return jax.shard_map(
        on_device,
        mesh=fine,
        in_specs=(both,) * 6 + (P(), P(), P()),
        out_specs=(both, P(blk + head, None)),
        check_vma=False,
    )
```
